32 devices in a mesh: groups: 2 (over x), atom: 16 (over z, y, core).
Axes of the slice: x: 2, y: 2, z: 4, core: 2. Of those that a mesh axis runs over, the one named last changes fastest.
Arguments:
- factors: bfloat16 [128, 128, 6144], P(('groups', 'atom')), parts along dimension 0, may hold values from -6 to 6
- block_sizes: int32 [128], P(('groups', 'atom')), parts along dimension 0, may hold values from 1 to 128, 6144 in all
- trial_vectors: bfloat16 [128, 128, 128], P(('groups', 'atom')), parts along dimension 0, may hold values from -0.5 to 0.5
- pair_list: int32 [2048, 2], P(('groups', 'atom')), parts along dimension 0, may hold values from 0 to 63, as said below
Outputs:
- kblocks: bfloat16 [2048, 128, 128], P(('groups', 'atom')), parts along dimension 0
- sigma: bfloat16 [128, 128, 128], P(('groups', 'atom')), parts along dimension 0
The draws below stay inside these ranges and needn't reach their ends.
There are 2 independent parts, one for each index of `groups`. The reference program is written for one: setup_inputs(seed, part) draws one part's arguments, and reference() takes and returns one part's arrays. A program takes and returns all parts, laid end to end along the dimension named above; each array names one. Nothing has to cross between parts.
Inputs may be any that keep to these rules, and one draw needn't show every extreme that they name: `pair_list`: the first block of each pair belongs to the owner whose rows hold the pair (pair p on owner p // 64, blocks a on owner a // 4); the second block's owner is that owner or up to 2 owners after it, never past the last. Pairs may repeat. `block_sizes`: their sum over a cluster is 6144.
All inputs are finite; a program needn't handle non-finite values. No bound on the sum of `block_sizes` on one device may be relied on, other than what follows from the above.
Results may differ from the reference program's by a relative error of at most 0.005.
Values may be sent and summed in bfloat16 or wider, within the bound.
A program may use at most 128 MiB of HBM per device.

```python
import math
import jax
import jax.numpy as jnp
import numpy as np
from jax import lax

NB = 128
NAUX = 6144
NVEC = 128
REACH = 2
BLK_DEV = 4
PAIR_DEV = 64
NBLOCKS = 64
NPAIRS = 1024


def draw_pair_list(key, part):
    key = jax.random.fold_in(key, 7)
    key_first, key_offset, key_second = jax.random.split(key, 3)
    rows = jnp.arange(NPAIRS, dtype=jnp.int32)
    owner = rows // PAIR_DEV
    owners = NBLOCKS // BLK_DEV
    first = owner * BLK_DEV + jax.random.randint(key_first, (NPAIRS,), 0, BLK_DEV)
    offset = jax.random.randint(key_offset, (NPAIRS,), 0, REACH + 1)
    target = jnp.minimum(owner + offset, owners - 1)
    second = target * BLK_DEV + jax.random.randint(key_second, (NPAIRS,), 0, BLK_DEV)
    return jnp.stack([first, second], axis=1).astype(jnp.int32)


def level_of(own_key, shape, cuts, least, largest):
    gain, own = 1.0, jax.random.fold_in(own_key, 6)
    for dim, parts in cuts:
        draws = jnp.exp(jax.random.uniform(jax.random.fold_in(own, dim), (parts,), jnp.float32, least / len(cuts), largest / len(cuts)))
        gain = gain * jnp.repeat(draws, shape[dim] // parts).reshape([-1 if axis == dim else 1 for axis in range(len(shape))])
    return gain


def length_profile(amount, total, bound, skew):
    weights = [(1 << 20) // math.isqrt(standing ** skew) + 1 for standing in range(2, amount + 1)]
    surplus, given = total - bound - (amount - 1), [1] * (amount - 1)
    while surplus > 0:
        candidates = [i for i in range(amount - 1) if given[i] < bound]
        whole, budget = sum([weights[i] for i in candidates]), surplus
        for i in candidates:
            more = min(bound - given[i], max(1, budget * weights[i] // whole), surplus)
            given[i] = given[i] + more
            surplus = surplus - more
    return np.array([bound] + given)


def uneven(stream_key, amount, total, most, slope):
    if amount == 2:
        one = jax.random.randint(stream_key, (), max(1, total - most), min(most, total - 1) + 1)
        return jnp.stack([one, total - one])
    sizes = jnp.asarray(length_profile(amount, total, most, slope), jnp.int32)
    couples = (amount - 1) // 2
    donor, sink = sizes[1:1 + 2 * couples:2], sizes[2:2 + 2 * couples:2]
    margin = jnp.minimum(donor - 1, most - sink)
    shifted = jax.random.randint(jax.random.fold_in(stream_key, 1), (couples,), 0, 1 << 20) % (margin + 1)
    sizes = sizes.at[1:1 + 2 * couples:2].set(donor - shifted).at[2:2 + 2 * couples:2].set(sink + shifted)
    return sizes[jax.random.permutation(jax.random.fold_in(stream_key, 2), amount)]


def scatter_about(rng, extent, deviation, most, cuts=(), held_as=jnp.bfloat16):
    drawn = jax.random.normal(rng, extent, jnp.float32) * deviation
    if len(cuts) > 0:
        drawn = level_of(rng, extent, cuts, -0.22, 0.18) * drawn
    return jnp.clip(drawn, min=-most, max=most).astype(held_as)


def setup_inputs(seed: int = 0, part: int = 0) -> dict:
    seeds = jax.random.split(jax.random.key(seed), 5)
    own_keys = jax.random.split(jax.random.fold_in(seeds[4], part), 5)
    return {
        "factors": scatter_about(own_keys[0], (NBLOCKS, NB, NAUX), 1.0, 6.0, ((0, 16),)),
        "block_sizes": uneven(own_keys[1], NBLOCKS, NBLOCKS * NB * 3 // 4, NB, 1).astype(jnp.int32),
        "trial_vectors": scatter_about(own_keys[2], (NBLOCKS, NB, NVEC), NB ** -0.5, 0.5, ((0, 16),)),
        "pair_list": draw_pair_list(jax.random.fold_in(jax.random.fold_in(seeds[4], part), 71), part),
    }


def reference(factors, block_sizes, trial_vectors, pair_list):
    rows = jnp.arange(NB, dtype=jnp.int32)
    keep = (rows[None, :] < block_sizes[:, None]).astype(factors.dtype)
    masked = factors * keep[:, :, None]
    scale = 1.0 / math.sqrt(NAUX)

    def one_pair(pair):
        left = masked[pair[0]]
        right = masked[pair[1]]
        return (jnp.dot(left, right.T, preferred_element_type=jnp.float32) * scale).astype(jnp.bfloat16)
    kblocks = lax.map(one_pair, pair_list)
    kfloat = kblocks.astype(jnp.float32)
    vfloat = trial_vectors.astype(jnp.float32)
    first = pair_list[:, 0]
    second = pair_list[:, 1]
    different = (first != second).astype(jnp.float32)
    forward = jnp.einsum('pij,pjk->pik', kfloat, vfloat[second])
    backward = jnp.einsum('pij,pik->pjk', kfloat, vfloat[first]) * different[:, None, None]
    sigma = jax.ops.segment_sum(forward, first, NBLOCKS) + jax.ops.segment_sum(backward, second, NBLOCKS)
    return (kblocks, sigma.astype(jnp.bfloat16))
```

```python
import math

import jax
import jax.numpy as jnp
from jax import lax
from jax.sharding import PartitionSpec as P

REACH = 2
CHUNKS = 2


def side(i):
    return (i // 2) % 2


def moved(value, pairs):
    return lax.ppermute(value, "atom", pairs)


def times(left, right):
    return lax.dot_general(left, right, (((1,), (1,)), ((), ())), preferred_element_type=jnp.float32)


def on_device(factors, block_sizes, trial_vectors, pair_list):
    count, width, depth = factors.shape
    rows = count * width
    half = depth // 2
    scale = 1.0 / math.sqrt(depth)
    devices = lax.axis_size("atom")
    ring = range(devices)
    me = lax.axis_index("atom")
    y = (me // 2) % 2
    core = me % 2
    bf16 = jnp.bfloat16

    flat = factors.reshape(rows, depth)
    keep = lax.dynamic_slice_in_dim(flat, y * half, half, 1)
    other = lax.dynamic_slice_in_dim(flat, (1 - y) * half, half, 1)

    step = rows // CHUNKS
    swap = [(i, i ^ 2) for i in ring]
    peers = [moved(other[j * step : (j + 1) * step], swap) for j in range(CHUNKS)]
    far = [(i, i - 4) for i in ring if side(i) == 0 and i >= 4]
    far += [(i, i + 4) for i in ring if side(i) == 1 and i + 4 < devices]
    outer = moved(keep, far)
    right = moved(flat, [(i, i - 1) for i in ring if i % 2 == 1])
    own_cross = moved(keep, [(i, i + 1) for i in ring if side(i) == 1 and i % 2 == 0])
    right_keep = lax.dynamic_slice_in_dim(right, y * half, half, 1)
    early = jnp.where(y == core, jnp.where(core == 0, right_keep, own_cross), jnp.zeros((), bf16))
    late = moved(
        outer,
        [(i, i + 1) for i in ring if side(i) == 0 and i % 2 == 0]
        + [(i, i - 1) for i in ring if side(i) == 1 and i % 2 == 1],
    )

    vectors, sizes = [trial_vectors], [block_sizes]
    for by in range(1, REACH + 1):
        back = [(i, i - by) for i in ring if i - by >= 0]
        vectors.append(moved(trial_vectors, back))
        sizes.append(moved(block_sizes, back))
    window_vectors = jnp.concatenate(vectors, axis=0)
    window_sizes = jnp.concatenate(sizes, axis=0)

    gram_own = times(flat, flat) * scale
    gram_right = times(flat, right) * scale

    natural, turned, cross_natural, cross_turned = [], [], [], []
    for peer in peers:
        with_own = times(peer, keep) * scale
        with_outer = times(peer, outer) * scale
        with_cross = (times(peer, early) + times(peer, late)) * scale
        natural.append(moved(jnp.where(y == 0, with_outer, with_own).astype(bf16), swap))
        from_far = moved(
            with_outer.astype(bf16), [(i, i - 4) for i in ring if side(i) == 1 and i >= 4]
        )
        turned.append(jnp.where(y == 0, with_own, from_far.astype(jnp.float32)))
        cross = with_cross.astype(bf16)
        cross_natural.append(moved(cross, [(i, i ^ 2) for i in ring if i % 2 == 1]))
        cross_turned.append(
            moved(
                cross,
                [(i, i + 1) for i in ring if i % 4 == 0]
                + [(i, i - 3) for i in ring if i % 4 == 2 and i >= 3],
            )
        )

    def joined(pieces):
        return jnp.concatenate(pieces, axis=0).astype(jnp.float32)

    gram_two = joined(natural) + joined(turned).T
    gram_odd = joined(cross_natural) + joined(cross_turned).T
    gram_one = jnp.where(core == 0, gram_right, gram_odd)
    gram = jnp.concatenate([gram_own, gram_one, gram_two], axis=1)

    slots = (REACH + 1) * count
    place = jnp.arange(width, dtype=jnp.int32)
    row_real = (place[None, :] < block_sizes[:, None]).reshape(rows, 1)
    column_real = (place[None, :] < window_sizes[:, None]).reshape(1, slots * width)
    gram = jnp.where(row_real & column_real, gram, 0.0).astype(bf16)
    gram_half = gram.reshape(count, width, slots, width).transpose(0, 2, 1, 3)

    start = me * count
    local_first = pair_list[:, 0] - start
    local_second = pair_list[:, 1] - start
    different = (pair_list[:, 0] != pair_list[:, 1]).astype(jnp.float32)
    npairs = pair_list.shape[0]
    first_hot = (local_first[:, None] == jnp.arange(count, dtype=jnp.int32)[None, :]).astype(
        jnp.float32
    )
    second_hot = (local_second[:, None] == jnp.arange(slots, dtype=jnp.int32)[None, :]).astype(
        jnp.float32
    )
    pair_hot = first_hot[:, :, None] * second_hot[:, None, :]
    select = pair_hot.reshape(npairs, count * slots).astype(bf16)
    picked = jnp.dot(
        select, gram_half.reshape(count * slots, width * width), preferred_element_type=jnp.float32
    )
    kblocks = picked.astype(bf16).reshape(npairs, width, width)
    pair_count = jnp.sum(pair_hot, axis=0)
    cross_count = jnp.sum(pair_hot * different[:, None, None], axis=0)
    forward = jnp.einsum(
        "abij,bjk->abik", gram_half, window_vectors, preferred_element_type=jnp.float32
    )
    backward = jnp.einsum(
        "abij,aik->abjk", gram_half, trial_vectors, preferred_element_type=jnp.float32
    )
    own_terms = jnp.sum(pair_count[:, :, None, None] * forward, axis=1)
    slot_terms = jnp.sum(cross_count[:, :, None, None] * backward, axis=0)
    total = own_terms + slot_terms[0:count]
    for by in range(1, REACH + 1):
        ahead = [(i, i + by) for i in ring if i + by < devices]
        total = total + moved(slot_terms[by * count : (by + 1) * count], ahead)
    return (kblocks, total.astype(bf16))


def solution(mesh):
    return jax.shard_map(
        on_device,
        mesh=mesh,
        in_specs=(
            P(("groups", "atom"), None, None),
            P(("groups", "atom")),
            P(("groups", "atom"), None, None),
            P(("groups", "atom"), None),
        ),
        out_specs=(P(("groups", "atom"), None, None), P(("groups", "atom"), None, None)),
        check_vma=False,
    )
```

```python
import functools
import math

import jax
import jax.numpy as jnp
from jax import lax
from jax.experimental import pallas as pl
from jax.experimental.pallas import tpu as pltpu
from jax.sharding import PartitionSpec as P

REACH = 2
PARTS = 2
BF16 = jnp.bfloat16
F32 = jnp.float32


def gram_kernel(
    devices, factors, sizes, vectors, pairs, gram, sigma,
    own, peer, outer, cross, right, window, acc,
    with_own, with_outer, with_cross, back_two, turned_two, back_one, turned_one,
    terms, got_terms, sums,
    load_sem, send_sem, recv_sem,
):
    rows, depth = own.shape
    half = depth // 2
    count = vectors.shape[0]
    width = rows // count
    slots = (REACH + 1) * count
    step = rows // PARTS
    scale = 1.0 / math.sqrt(depth)
    me = lax.axis_index("atom")
    y = lax.rem(lax.div(me, 2), 2)
    core = lax.rem(me, 2)
    lower, upper = y == 0, y == 1
    even, odd = core == 0, core == 1
    swap = me + 2 - 4 * y
    mate = me + 1 - 2 * core
    kept = pl.multiple_of(y * half, 128)
    given = pl.multiple_of((1 - y) * half, 128)

    used = {}

    def copy(name, source, target, device):
        at = used.setdefault(name, len(used))
        return pltpu.make_async_remote_copy(
            src_ref=source, dst_ref=target, send_sem=send_sem.at[at], recv_sem=recv_sem.at[at],
            device_id={"atom": device}, device_id_type=pl.DeviceIdType.MESH,
        )

    def part(j):
        return pl.ds(j * step, step)

    def load(j):
        return pltpu.make_async_copy(factors.at[part(j)], own.at[part(j)], load_sem.at[j])

    for j in range(PARTS):
        load(j).start()

    barrier = pltpu.get_barrier_semaphore()
    for by in (-4, -3, -2, -1, 1, 2, 3, 4):
        @pl.when((me + by >= 0) & (me + by < devices))
        def _(by=by):
            pl.semaphore_signal(
                barrier, inc=1, device_id={"atom": me + by}, device_id_type=pl.DeviceIdType.MESH
            )
    pl.semaphore_wait(barrier, jnp.minimum(me, 4) + jnp.minimum(devices - 1 - me, 4))

    def peer_copy(j):
        return copy(("peer", j), own.at[part(j), pl.ds(given, half)], peer.at[part(j)], swap)

    far = me - 4 + 8 * y
    far_out = (lower & (me >= 4)) | (upper & (me + 4 < devices))
    far_in = (lower & (me + 4 < devices)) | (upper & (me >= 4))

    def outer_copy(j):
        return copy(("outer", j), own.at[part(j), pl.ds(kept, half)], outer.at[part(j)], far)

    def cross_copy_own(j):
        return copy(("cross", j), own.at[part(j), pl.ds(kept, half)], cross.at[part(j)], mate)

    def cross_copy_outer(j):
        return copy(("cross", j), outer.at[part(j)], cross.at[part(j)], mate)

    def right_copy(j):
        return copy(("right", j), own.at[part(j)], right.at[part(j)], me - 1)

    def window_copy(by):
        return copy(("window", by), vectors, window.at[by - 1], me - by)

    wide = 512
    for j in range(PARTS):
        load(j).wait()

        @pl.loop(0, depth // wide)
        def _(c, j=j):
            at = pl.ds(pl.multiple_of(c * wide, wide), wide)
            for b in range(step // width):
                block = j * (step // width) + b
                lines = pl.ds(block * width, width)
                real = lax.broadcasted_iota(jnp.int32, (width, wide), 0) < sizes[block]
                tile = own[lines, at].astype(F32)
                own[lines, at] = jnp.where(real, tile, 0.0).astype(BF16)

        peer_copy(j).start()
        pl.when(far_out)(lambda j=j: outer_copy(j).start())
        pl.when(y != core)(lambda j=j: cross_copy_own(j).start())
    for j in range(PARTS):
        pl.when(odd)(lambda j=j: right_copy(j).start())
    for by in range(1, REACH + 1):
        pl.when(me >= by)(lambda by=by: window_copy(by).start())

    @pl.when(~far_in)
    def _():
        outer[...] = jnp.zeros_like(outer)

    @pl.when(upper & (me + 4 >= devices))
    def _():
        turned_two[...] = jnp.zeros_like(turned_two)

    @pl.when(odd & upper & (me + 3 >= devices))
    def _():
        turned_one[...] = jnp.zeros_like(turned_one)

    for by in range(1, REACH + 1):
        @pl.when(me + by >= devices)
        def _(by=by):
            window[by - 1] = jnp.zeros_like(window[by - 1])

    def product(left, lines, left_from, other, other_from, length, piece):
        acc[...] = jnp.zeros_like(acc)

        @pl.loop(0, length // piece)
        def _(k):
            a = left[lines, pl.ds(pl.multiple_of(left_from + k * piece, 128), piece)]
            b = other[:, pl.ds(pl.multiple_of(other_from + k * piece, 128), piece)]
            acc[...] += lax.dot_general(a, b, (((1,), (1,)), ((), ())), preferred_element_type=F32)

    piece = half // 3

    def keep_blocks(j, slot):
        for a in range(step // width):
            for b in range(count):
                tile = acc[a * width : (a + 1) * width, b * width : (b + 1) * width] * scale
                gram[j * (step // width) + a, slot * count + b] = tile.astype(BF16)

    for j in range(PARTS):
        product(own, part(j), 0, own, 0, depth, piece)
        keep_blocks(j, 0)

    @pl.when(even)
    def _():
        for j in range(PARTS):
            right_copy(j).wait_recv()
        for j in range(PARTS):
            product(own, part(j), 0, right, 0, depth, piece)
            keep_blocks(j, 1)

    local = pairs[...] - me * count
    code = local[:, 0:1] * slots + local[:, 1:2]
    places = lax.broadcasted_iota(jnp.int32, (pairs.shape[0], 128), 1)
    hot = jnp.where(code == places, 1.0, 0.0).astype(F32)
    apart = jnp.where(local[:, 0:1] != local[:, 1:2], 1.0, 0.0).astype(F32)
    pair_count = jnp.sum(hot, axis=0, keepdims=True)
    cross_count = jnp.sum(hot * apart, axis=0, keepdims=True)

    def two_copy(j, source):
        return copy(("two", j), source.at[part(j)], back_two.at[part(j)], swap)

    def far_copy(j):
        return copy(("far", j), with_outer.at[part(j)], turned_two.at[part(j)], me - 4)

    def one_copy(j):
        return copy(("one", j), with_cross.at[part(j)], back_one.at[part(j)], swap)

    def skew_copy(j):
        return copy(("skew", j), with_cross.at[part(j)], turned_one.at[part(j)], me + 1 - 4 * y)

    for j in range(PARTS):
        @pl.when(far_in)
        def _(j=j):
            outer_copy(j).wait_recv()
        pl.when(y == core)(lambda j=j: cross_copy_outer(j).start())
        peer_copy(j).wait_recv()
        product(peer, part(j), 0, own, kept, half, piece)

        @pl.when(lower)
        def _(j=j):
            turned_two[part(j)] = (acc[...] * scale).astype(BF16)

        @pl.when(upper)
        def _(j=j):
            with_own[part(j)] = (acc[...] * scale).astype(BF16)
            two_copy(j, with_own).start()

    far_back = upper & (me >= 4)
    skew_out = even & (lower | (me >= 3))
    skew_in = odd & (lower | (me + 3 < devices))
    for j in range(PARTS):
        product(peer, part(j), 0, outer, 0, half, piece)
        with_outer[part(j)] = (acc[...] * scale).astype(BF16)
        pl.when(lower)(lambda j=j: two_copy(j, with_outer).start())
        pl.when(far_back)(lambda j=j: far_copy(j).start())
    for j in range(PARTS):
        cross_copy_own(j).wait_recv()
    for j in range(PARTS):
        product(peer, part(j), 0, cross, 0, half, piece)
        with_cross[part(j)] = (acc[...] * scale).astype(BF16)
        pl.when(odd)(lambda j=j: one_copy(j).start())
        pl.when(skew_out)(lambda j=j: skew_copy(j).start())

    for j in range(PARTS):
        two_copy(j, with_own).wait_recv()
        pl.when(upper & (me + 4 < devices))(lambda j=j: far_copy(j).wait_recv())

    def settle(natural, turned, slot):
        for a in range(count):
            for b in range(count):
                ra, rb = slice(a * width, (a + 1) * width), slice(b * width, (b + 1) * width)
                tile = natural[ra, rb].astype(F32) + turned[rb, ra].astype(F32).T
                gram[a, slot * count + b] = tile.astype(BF16)

    settle(back_two, turned_two, 2)

    @pl.when(odd)
    def _():
        for j in range(PARTS):
            one_copy(j).wait_recv()
            pl.when(skew_in)(lambda j=j: skew_copy(j).wait_recv())
        settle(back_one, turned_one, 1)

    for by in range(1, REACH + 1):
        pl.when(me + by < devices)(lambda by=by: window_copy(by).wait_recv())

    def backward(slot):
        total = jnp.zeros((width, vectors.shape[2]), F32)
        for a in range(count):
            term = lax.dot_general(
                gram[a, slot], vectors[a], (((0,), (0,)), ((), ())), preferred_element_type=F32
            )
            at = a * slots + slot
            total = total + term * cross_count[:, at : at + 1]
        return total

    def terms_copy(by):
        return copy(("terms", by), terms.at[by - 1], got_terms.at[by - 1], me + by)

    for by in range(REACH, 0, -1):
        for b in range(count):
            terms[by - 1, b] = backward(by * count + b).astype(BF16)
        pl.when(me + by < devices)(lambda by=by: terms_copy(by).start())

    totals = []
    for a in range(count):
        total = backward(a)
        for slot in range(slots):
            column = vectors[slot] if slot < count else window[slot // count - 1, slot % count]
            at = a * slots + slot
            term = jnp.dot(gram[a, slot], column, preferred_element_type=F32)
            total = total + term * pair_count[:, at : at + 1]
        sums[a * width : (a + 1) * width] = total
    for by in range(1, REACH + 1):
        @pl.when(me >= by)
        def _(by=by):
            terms_copy(by).wait_recv()
            for a in range(count):
                lines = slice(a * width, (a + 1) * width)
                sums[lines] += got_terms[by - 1, a].astype(F32)
    for a in range(count):
        sigma[a] = sums[a * width : (a + 1) * width].astype(BF16)

    for j in range(PARTS):
        peer_copy(j).wait_send()
        pl.when(far_out)(lambda j=j: outer_copy(j).wait_send())
        cross_copy_own(j).wait_send()
        pl.when(odd)(lambda j=j: right_copy(j).wait_send())
        two_copy(j, with_own).wait_send()
        pl.when(far_back)(lambda j=j: far_copy(j).wait_send())
        pl.when(odd)(lambda j=j: one_copy(j).wait_send())
        pl.when(skew_out)(lambda j=j: skew_copy(j).wait_send())
    for by in range(1, REACH + 1):
        pl.when(me >= by)(lambda by=by: window_copy(by).wait_send())
        pl.when(me + by < devices)(lambda by=by: terms_copy(by).wait_send())


def pick_kernel(pairs, gram, kblocks, sem):
    count, slots = gram.shape[0], gram.shape[1]
    npairs = kblocks.shape[0]
    start = lax.axis_index("atom") * count

    @pl.loop(0, npairs)
    def _(p):
        pltpu.make_async_copy(
            gram.at[pairs[p, 0] - start, pairs[p, 1] - start], kblocks.at[p], sem
        ).start()

    pltpu.make_async_copy(kblocks, kblocks, sem).wait()


def on_device(factors, block_sizes, trial_vectors, pair_list):
    count, width, depth = factors.shape
    rows = count * width
    half = depth // 2
    slots = (REACH + 1) * count
    devices = lax.axis_size("atom")
    copies = 8 * PARTS + 2 * REACH
    vmem, smem, hbm = pltpu.VMEM, pltpu.SMEM, pl.ANY
    nvec = trial_vectors.shape[2]
    gram, sigma = pl.pallas_call(
        functools.partial(gram_kernel, devices),
        out_shape=(
            jax.ShapeDtypeStruct((count, slots, width, width), BF16),
            jax.ShapeDtypeStruct(trial_vectors.shape, BF16),
        ),
        in_specs=[pl.BlockSpec(memory_space=s) for s in (hbm, smem, vmem, vmem)],
        out_specs=(pl.BlockSpec(memory_space=vmem), pl.BlockSpec(memory_space=vmem)),
        scratch_shapes=[
            pltpu.VMEM((rows, depth), BF16),
            pltpu.VMEM((rows, half), BF16),
            pltpu.VMEM((rows, half), BF16),
            pltpu.VMEM((rows, half), BF16),
            pltpu.VMEM((rows, depth), BF16),
            pltpu.VMEM((REACH, count, width, nvec), BF16),
            pltpu.VMEM((rows // PARTS, rows), F32),
        ]
        + [pltpu.VMEM((rows, rows), BF16)] * 7
        + [
            pltpu.VMEM((REACH, count, width, nvec), BF16),
            pltpu.VMEM((REACH, count, width, nvec), BF16),
            pltpu.VMEM((rows, nvec), F32),
            pltpu.SemaphoreType.DMA((PARTS,)),
            pltpu.SemaphoreType.DMA((copies,)),
            pltpu.SemaphoreType.DMA((copies,)),
        ],
        compiler_params=pltpu.CompilerParams(
            collective_id=0, has_side_effects=True, vmem_limit_bytes=56 * 1024 * 1024
        ),
    )(factors.reshape(rows, depth), block_sizes, trial_vectors, pair_list)
    kblocks = pl.pallas_call(
        pick_kernel,
        out_shape=jax.ShapeDtypeStruct((pair_list.shape[0], width, width), BF16),
        in_specs=[pl.BlockSpec(memory_space=smem), pl.BlockSpec(memory_space=vmem)],
        out_specs=pl.BlockSpec(memory_space=hbm),
        scratch_shapes=[pltpu.SemaphoreType.DMA],
        compiler_params=pltpu.CompilerParams(vmem_limit_bytes=32 * 1024 * 1024),
    )(pair_list, gram)
    return (kblocks, sigma)


def solution(mesh):
    return jax.shard_map(
        on_device,
        mesh=mesh,
        in_specs=(
            P(("groups", "atom"), None, None),
            P(("groups", "atom")),
            P(("groups", "atom"), None, None),
            P(("groups", "atom"), None),
        ),
        out_specs=(P(("groups", "atom"), None, None), P(("groups", "atom"), None, None)),
        check_vma=False,
    )
```

```python
import functools
import math

import jax
import jax.numpy as jnp
from jax import lax
from jax.experimental import pallas as pl
from jax.experimental.pallas import tpu as pltpu
from jax.sharding import PartitionSpec as P

REACH = 2
PARTS = 2
BF16 = jnp.bfloat16
F32 = jnp.float32


def gram_kernel(
    devices, factors, sizes, vectors, pairs, pairs_at, kblocks, sigma,
    gram, picked, mark, window_mark,
    own, peer, outer, cross, right, window, acc,
    with_own, with_outer, with_cross, back_two, turned_two, back_one, turned_one,
    terms, got_terms, sums,
    load_sem, out_sem, send_sem, recv_sem,
):
    rows, depth = own.shape
    half = depth // 2
    count = vectors.shape[0]
    width = rows // count
    slots = (REACH + 1) * count
    step = rows // PARTS
    scale = 1.0 / math.sqrt(depth)
    me = lax.axis_index("atom")
    y = lax.rem(lax.div(me, 2), 2)
    core = lax.rem(me, 2)
    lower, upper = y == 0, y == 1
    even, odd = core == 0, core == 1
    swap = me + 2 - 4 * y
    mate = me + 1 - 2 * core
    kept = pl.multiple_of(y * half, 128)
    given = pl.multiple_of((1 - y) * half, 128)

    used = {}

    def copy(name, source, target, device):
        at = used.setdefault(name, len(used))
        return pltpu.make_async_remote_copy(
            src_ref=source, dst_ref=target, send_sem=send_sem.at[at], recv_sem=recv_sem.at[at],
            device_id={"atom": device}, device_id_type=pl.DeviceIdType.MESH,
        )

    def part(j):
        return pl.ds(j * step, step)

    def load(j):
        return pltpu.make_async_copy(factors.at[part(j)], own.at[part(j)], load_sem.at[j])

    for j in range(PARTS):
        load(j).start()

    barrier = pltpu.get_barrier_semaphore()
    for by in (-4, -3, -2, -1, 1, 2, 3, 4):
        @pl.when((me + by >= 0) & (me + by < devices))
        def _(by=by):
            pl.semaphore_signal(
                barrier, inc=1, device_id={"atom": me + by}, device_id_type=pl.DeviceIdType.MESH
            )
    pl.semaphore_wait(barrier, jnp.minimum(me, 4) + jnp.minimum(devices - 1 - me, 4))

    def peer_copy(j):
        return copy(("peer", j), factors.at[part(j), pl.ds(given, half)], peer.at[part(j)], swap)

    far = me - 4 + 8 * y
    far_out = (lower & (me >= 4)) | (upper & (me + 4 < devices))
    far_in = (lower & (me + 4 < devices)) | (upper & (me >= 4))

    def outer_copy(j):
        return copy(("outer", j), factors.at[part(j), pl.ds(kept, half)], outer.at[part(j)], far)

    def cross_copy_own(j):
        return copy(("cross", j), factors.at[part(j), pl.ds(kept, half)], cross.at[part(j)], mate)

    def cross_copy_outer(j):
        return copy(("cross", j), outer.at[part(j)], cross.at[part(j)], mate)

    def right_copy(j):
        return copy(("right", j), factors.at[part(j)], right.at[part(j)], me - 1)

    def window_copy(by, source=vectors):
        return copy(("window", by), source, window.at[by - 1], me - 2 if by == 2 else mate)

    def mark_copy(by):
        return copy(("mark", by), mark, window_mark.at[by - 1], me - by)

    for b in range(count):
        real = lax.broadcasted_iota(jnp.int32, mark.shape[1:], 1) < sizes[b]
        mark[b] = jnp.where(real, 1.0, 0.0).astype(BF16)
    for j in range(PARTS):
        peer_copy(j).start()
        pl.when(far_out)(lambda j=j: outer_copy(j).start())
        pl.when(y != core)(lambda j=j: cross_copy_own(j).start())
        if j == 0:
            for by in range(1, REACH + 1):
                pl.when(me >= by)(lambda by=by: mark_copy(by).start())
    for j in range(PARTS):
        pl.when(odd)(lambda j=j: right_copy(j).start())
    for by in range(1, REACH + 1):
        pl.when(me >= 2 if by == 2 else odd)(lambda by=by: window_copy(by).start())

    @pl.when(~far_in)
    def _():
        outer[...] = jnp.zeros_like(outer)

    @pl.when(upper & (me + 4 >= devices))
    def _():
        turned_two[...] = jnp.zeros_like(turned_two)

    @pl.when(odd & upper & (me + 3 >= devices))
    def _():
        turned_one[...] = jnp.zeros_like(turned_one)

    for by in range(1, REACH + 1):
        @pl.when(me + by >= devices)
        def _(by=by):
            window[by - 1] = jnp.zeros_like(window[by - 1])
            window_mark[by - 1] = jnp.zeros_like(window_mark[by - 1])

    for j in range(PARTS):
        load(j).wait()

    def product(left, lines, left_from, other, other_from, length, piece):
        acc[...] = jnp.zeros_like(acc)

        @pl.loop(0, length // piece)
        def _(k):
            a = left[lines, pl.ds(pl.multiple_of(left_from + k * piece, 128), piece)]
            b = other[:, pl.ds(pl.multiple_of(other_from + k * piece, 128), piece)]
            acc[...] += lax.dot_general(a, b, (((1,), (1,)), ((), ())), preferred_element_type=F32)

    piece = half // 3

    def real_only(tile, a, slot, b):
        lines = lax.broadcasted_iota(jnp.int32, (width, width), 0) < sizes[a]
        columns = mark[b, 0:1] if slot == 0 else window_mark[slot - 1, b, 0:1]
        return (jnp.where(lines, tile, 0.0) * columns.astype(F32)).astype(BF16)

    def keep_blocks(j, slot):
        for a in range(step // width):
            for b in range(count):
                tile = acc[a * width : (a + 1) * width, b * width : (b + 1) * width] * scale
                at = j * (step // width) + a
                gram[at, slot * count + b] = real_only(tile, at, slot, b)

    for j in range(PARTS):
        product(own, part(j), 0, own, 0, depth, piece)
        keep_blocks(j, 0)

    for by in range(1, REACH + 1):
        pl.when(me + by < devices)(lambda by=by: mark_copy(by).wait_recv())

    @pl.when(even)
    def _():
        for j in range(PARTS):
            right_copy(j).wait_recv()
        for j in range(PARTS):
            product(own, part(j), 0, right, 0, depth, piece)
            keep_blocks(j, 1)

    local = pairs[...] - me * count
    code = local[0:1] * slots + local[1:2]
    places = lax.broadcasted_iota(jnp.int32, (count * slots, pairs.shape[1]), 0)
    hot = jnp.where(code == places, 1.0, 0.0).astype(F32)
    apart = jnp.where(local[0:1] != local[1:2], 1.0, 0.0).astype(F32)
    pair_count = jnp.sum(hot, axis=1, keepdims=True)
    cross_count = jnp.sum(hot * apart, axis=1, keepdims=True)

    def two_copy(j, source):
        return copy(("two", j), source.at[part(j)], back_two.at[part(j)], swap)

    def far_copy(j):
        return copy(("far", j), with_outer.at[part(j)], turned_two.at[part(j)], me - 4)

    def one_copy(j):
        return copy(("one", j), with_cross.at[part(j)], back_one.at[part(j)], swap)

    def skew_copy(j):
        return copy(("skew", j), with_cross.at[part(j)], turned_one.at[part(j)], me + 1 - 4 * y)

    def turn_own(j):
        product(peer, part(j), 0, own, kept, half, piece)
        turned_two[part(j)] = (acc[...] * scale).astype(BF16)

    for j in range(PARTS):
        @pl.when(far_in)
        def _(j=j):
            outer_copy(j).wait_recv()
        pl.when(y == core)(lambda j=j: cross_copy_outer(j).start())
        peer_copy(j).wait_recv()

        @pl.when(upper)
        def _(j=j):
            product(peer, part(j), 0, own, kept, half, piece)
            with_own[part(j)] = (acc[...] * scale).astype(BF16)
            two_copy(j, with_own).start()

        if j < PARTS - 1:
            pl.when(lower)(lambda j=j: turn_own(j))

    far_back = upper & (me >= 4)
    skew_out = even & (lower | (me >= 3))
    skew_in = odd & (lower | (me + 3 < devices))
    @pl.when(lower)
    def _():
        for j in range(PARTS):
            product(peer, part(j), 0, outer, 0, half, piece)
            with_outer[part(j)] = (acc[...] * scale).astype(BF16)
            two_copy(j, with_outer).start()

    for j in range(PARTS):
        cross_copy_own(j).wait_recv()
    for j in range(PARTS):
        product(peer, part(j), 0, cross, 0, half, piece)
        with_cross[part(j)] = (acc[...] * scale).astype(BF16)
        pl.when(odd)(lambda j=j: one_copy(j).start())
        pl.when(skew_out)(lambda j=j: skew_copy(j).start())
    pl.when(lower)(lambda: turn_own(PARTS - 1))

    @pl.when(far_back)
    def _():
        for j in range(PARTS):
            product(peer, part(j), 0, outer, 0, half, piece)
            with_outer[part(j)] = (acc[...] * scale).astype(BF16)
            far_copy(j).start()

    passing = even & (me + 2 < devices)

    @pl.when(me + 2 < devices)
    def _():
        window_copy(2).wait_recv()

        @pl.when(even)
        def _():
            window_copy(1, window.at[1]).start()

    for j in range(PARTS):
        two_copy(j, with_own).wait_recv()
        pl.when(upper & (me + 4 < devices))(lambda j=j: far_copy(j).wait_recv())

    def settle(natural, turned, slot):
        for a in range(count):
            for b in range(count):
                ra, rb = slice(a * width, (a + 1) * width), slice(b * width, (b + 1) * width)
                tile = natural[ra, rb].astype(F32) + turned[rb, ra].astype(F32).T
                gram[a, slot * count + b] = real_only(tile, a, slot, b)

    def backward(slot):
        total = jnp.zeros((width, vectors.shape[2]), F32)
        for a in range(count):
            term = lax.dot_general(
                gram[a, slot], vectors[a], (((0,), (0,)), ((), ())), preferred_element_type=F32
            )
            at = a * slots + slot
            total = total + term * cross_count[at : at + 1]
        return total

    def terms_copy(by):
        return copy(("terms", by), terms.at[by - 1], got_terms.at[by - 1], me + by)

    def leave(by):
        for b in range(count):
            terms[by - 1, b] = backward(by * count + b).astype(BF16)
        pl.when(me + by < devices)(lambda: terms_copy(by).start())

    settle(back_two, turned_two, 2)

    leave(2)

    @pl.when(odd)
    def _():
        for j in range(PARTS):
            one_copy(j).wait_recv()
            pl.when(skew_in)(lambda j=j: skew_copy(j).wait_recv())
        settle(back_one, turned_one, 1)

    leave(1)

    @pl.loop(0, picked.shape[0])
    def _(p):
        a = jnp.clip(pairs_at[0, p] - me * count, 0, count - 1)
        b = jnp.clip(pairs_at[1, p] - me * count, 0, slots - 1)
        picked[p] = gram[a, b]

    result = pltpu.make_async_copy(picked, kblocks, out_sem)
    result.start()
    pl.when(me + 1 < devices)(lambda: window_copy(1).wait_recv())

    for a in range(count):
        total = backward(a)
        for slot in range(slots):
            column = vectors[slot] if slot < count else window[slot // count - 1, slot % count]
            at = a * slots + slot
            term = jnp.dot(gram[a, slot], column, preferred_element_type=F32)
            total = total + term * pair_count[at : at + 1]
        sums[a * width : (a + 1) * width] = total
    for by in range(1, REACH + 1):
        @pl.when(me >= by)
        def _(by=by):
            terms_copy(by).wait_recv()
            for a in range(count):
                lines = slice(a * width, (a + 1) * width)
                sums[lines] += got_terms[by - 1, a].astype(F32)
    for a in range(count):
        sigma[a] = sums[a * width : (a + 1) * width].astype(BF16)

    result.wait()
    for j in range(PARTS):
        peer_copy(j).wait_send()
        pl.when(far_out)(lambda j=j: outer_copy(j).wait_send())
        cross_copy_own(j).wait_send()
        pl.when(odd)(lambda j=j: right_copy(j).wait_send())
        two_copy(j, with_own).wait_send()
        pl.when(far_back)(lambda j=j: far_copy(j).wait_send())
        pl.when(odd)(lambda j=j: one_copy(j).wait_send())
        pl.when(skew_out)(lambda j=j: skew_copy(j).wait_send())
    for by in range(1, REACH + 1):
        pl.when(me >= 2 if by == 2 else odd | passing)(lambda by=by: window_copy(by).wait_send())
        pl.when(me >= by)(lambda by=by: mark_copy(by).wait_send())
        pl.when(me + by < devices)(lambda by=by: terms_copy(by).wait_send())


def on_device(factors, block_sizes, trial_vectors, pair_list):
    count, width, depth = factors.shape
    rows = count * width
    half = depth // 2
    slots = (REACH + 1) * count
    devices = lax.axis_size("atom")
    copies = 8 * PARTS + 3 * REACH
    vmem, smem, hbm = pltpu.VMEM, pltpu.SMEM, pl.ANY
    nvec = trial_vectors.shape[2]
    npairs = pair_list.shape[0]
    turned_list = pair_list.T
    return pl.pallas_call(
        functools.partial(gram_kernel, devices),
        out_shape=(
            jax.ShapeDtypeStruct((npairs, width, width), BF16),
            jax.ShapeDtypeStruct(trial_vectors.shape, BF16),
        ),
        in_specs=[pl.BlockSpec(memory_space=s) for s in (hbm, smem, vmem, vmem, smem)],
        out_specs=(pl.BlockSpec(memory_space=hbm), pl.BlockSpec(memory_space=vmem)),
        scratch_shapes=[
            pltpu.VMEM((count, slots, width, width), BF16),
            pltpu.VMEM((npairs, width, width), BF16),
            pltpu.VMEM((count, 16, width), BF16),
            pltpu.VMEM((REACH, count, 16, width), BF16),
            pltpu.VMEM((rows, depth), BF16),
            pltpu.VMEM((rows, half), BF16),
            pltpu.VMEM((rows, half), BF16),
            pltpu.VMEM((rows, half), BF16),
            pltpu.VMEM((rows, depth), BF16),
            pltpu.VMEM((REACH, count, width, nvec), BF16),
            pltpu.VMEM((rows // PARTS, rows), F32),
        ]
        + [pltpu.VMEM((rows, rows), BF16)] * 7
        + [
            pltpu.VMEM((REACH, count, width, nvec), BF16),
            pltpu.VMEM((REACH, count, width, nvec), BF16),
            pltpu.VMEM((rows, nvec), F32),
            pltpu.SemaphoreType.DMA((PARTS,)),
            pltpu.SemaphoreType.DMA,
            pltpu.SemaphoreType.DMA((copies,)),
            pltpu.SemaphoreType.DMA((copies,)),
        ],
        compiler_params=pltpu.CompilerParams(
            collective_id=0, has_side_effects=True, vmem_limit_bytes=56 * 1024 * 1024
        ),
    )(factors.reshape(rows, depth), block_sizes, trial_vectors, turned_list, turned_list)


def solution(mesh):
    return jax.shard_map(
        on_device,
        mesh=mesh,
        in_specs=(
            P(("groups", "atom"), None, None),
            P(("groups", "atom")),
            P(("groups", "atom"), None, None),
            P(("groups", "atom"), None),
        ),
        out_specs=(P(("groups", "atom"), None, None), P(("groups", "atom"), None, None)),
        check_vma=False,
    )
```

```python
import functools
import math

import jax
import jax.numpy as jnp
from jax import lax
from jax.experimental import pallas as pl
from jax.experimental.pallas import tpu as pltpu
from jax.sharding import PartitionSpec as P

REACH = 2
PARTS = 2
GROUP = 8
BF16 = jnp.bfloat16
F32 = jnp.float32


def gram_kernel(
    devices, factors, sizes, vectors, pairs, pairs_at, kblocks, sigma,
    gram, picked, mark, window_mark,
    own, peer, outer, cross, right, window, acc,
    with_own, with_outer, with_cross, back_two, turned_two, back_one, turned_one,
    terms, got_terms, sums,
    load_sem, out_sem, send_sem, recv_sem,
):
    rows, depth = own.shape
    half = depth // 2
    count = vectors.shape[0]
    width = rows // count
    slots = (REACH + 1) * count
    step = rows // PARTS
    scale = 1.0 / math.sqrt(depth)
    me = lax.axis_index("atom")
    y = lax.rem(lax.div(me, 2), 2)
    core = lax.rem(me, 2)
    lower, upper = y == 0, y == 1
    even, odd = core == 0, core == 1
    swap = me + 2 - 4 * y
    mate = me + 1 - 2 * core
    kept = pl.multiple_of(y * half, 128)
    given = pl.multiple_of((1 - y) * half, 128)

    used = {}

    def copy(name, source, target, device):
        at = used.setdefault(name, len(used))
        return pltpu.make_async_remote_copy(
            src_ref=source, dst_ref=target, send_sem=send_sem.at[at], recv_sem=recv_sem.at[at],
            device_id={"atom": device}, device_id_type=pl.DeviceIdType.MESH,
        )

    def part(j):
        return pl.ds(j * step, step)

    def load(j):
        return pltpu.make_async_copy(factors.at[part(j)], own.at[part(j)], load_sem.at[j])

    for j in range(PARTS):
        load(j).start()

    barrier = pltpu.get_barrier_semaphore()
    for by in (-4, -3, -2, -1, 1, 2, 3, 4):
        @pl.when((me + by >= 0) & (me + by < devices))
        def _(by=by):
            pl.semaphore_signal(
                barrier, inc=1, device_id={"atom": me + by}, device_id_type=pl.DeviceIdType.MESH
            )
    pl.semaphore_wait(barrier, jnp.minimum(me, 4) + jnp.minimum(devices - 1 - me, 4))

    def peer_copy(j):
        return copy(("peer", j), factors.at[part(j), pl.ds(given, half)], peer.at[part(j)], swap)

    far = me - 4 + 8 * y
    far_out = (lower & (me >= 4)) | (upper & (me + 4 < devices))
    far_in = (lower & (me + 4 < devices)) | (upper & (me >= 4))

    def outer_copy(j):
        return copy(("outer", j), factors.at[part(j), pl.ds(kept, half)], outer.at[part(j)], far)

    def cross_copy_own(j):
        return copy(("cross", j), factors.at[part(j), pl.ds(kept, half)], cross.at[part(j)], mate)

    def cross_copy_outer(j):
        return copy(("cross", j), outer.at[part(j)], cross.at[part(j)], mate)

    def right_copy(j):
        return copy(("right", j), factors.at[part(j)], right.at[part(j)], me - 1)

    def window_copy(by, source=vectors):
        return copy(("window", by), source, window.at[by - 1], me - 2 if by == 2 else mate)

    def mark_copy(by):
        return copy(("mark", by), mark, window_mark.at[by - 1], me - by)

    for b in range(count):
        real = lax.broadcasted_iota(jnp.int32, mark.shape[1:], 1) < sizes[b]
        mark[b] = jnp.where(real, 1.0, 0.0).astype(BF16)
    for j in range(PARTS):
        peer_copy(j).start()
        pl.when(far_out)(lambda j=j: outer_copy(j).start())
        pl.when(y != core)(lambda j=j: cross_copy_own(j).start())
        if j == 0:
            for by in range(1, REACH + 1):
                pl.when(me >= by)(lambda by=by: mark_copy(by).start())
    for j in range(PARTS):
        pl.when(odd)(lambda j=j: right_copy(j).start())
    for by in range(1, REACH + 1):
        pl.when(me >= 2 if by == 2 else odd)(lambda by=by: window_copy(by).start())

    @pl.when(~far_in)
    def _():
        outer[...] = jnp.zeros_like(outer)

    @pl.when(upper & (me + 4 >= devices))
    def _():
        turned_two[...] = jnp.zeros_like(turned_two)

    @pl.when(odd & upper & (me + 3 >= devices))
    def _():
        turned_one[...] = jnp.zeros_like(turned_one)

    for by in range(1, REACH + 1):
        @pl.when(me + by >= devices)
        def _(by=by):
            window[by - 1] = jnp.zeros_like(window[by - 1])
            window_mark[by - 1] = jnp.zeros_like(window_mark[by - 1])

    for j in range(PARTS):
        load(j).wait()

    def product(left, lines, left_from, other, other_from, length, piece):
        acc[...] = jnp.zeros_like(acc)

        @pl.loop(0, length // piece)
        def _(k):
            a = left[lines, pl.ds(pl.multiple_of(left_from + k * piece, 128), piece)]
            b = other[:, pl.ds(pl.multiple_of(other_from + k * piece, 128), piece)]
            acc[...] += lax.dot_general(a, b, (((1,), (1,)), ((), ())), preferred_element_type=F32)

    piece = half // 3

    def real_only(tile, a, slot, b):
        lines = lax.broadcasted_iota(jnp.int32, (width, width), 0) < sizes[a]
        columns = mark[b, 0:1] if slot == 0 else window_mark[slot - 1, b, 0:1]
        return (jnp.where(lines, tile, 0.0) * columns.astype(F32)).astype(BF16)

    def keep_blocks(j, slot):
        for a in range(step // width):
            for b in range(count):
                tile = acc[a * width : (a + 1) * width, b * width : (b + 1) * width] * scale
                at = j * (step // width) + a
                gram[at, slot * count + b] = real_only(tile, at, slot, b)

    for j in range(PARTS):
        product(own, part(j), 0, own, 0, depth, piece)
        keep_blocks(j, 0)

    for by in range(1, REACH + 1):
        pl.when(me + by < devices)(lambda by=by: mark_copy(by).wait_recv())

    @pl.when(even)
    def _():
        for j in range(PARTS):
            right_copy(j).wait_recv()
        for j in range(PARTS):
            product(own, part(j), 0, right, 0, depth, piece)
            keep_blocks(j, 1)

    local = pairs[...] - me * count
    code = local[0:1] * slots + local[1:2]
    places = lax.broadcasted_iota(jnp.int32, (count * slots, pairs.shape[1]), 0)
    hot = jnp.where(code == places, 1.0, 0.0).astype(F32)
    apart = jnp.where(local[0:1] != local[1:2], 1.0, 0.0).astype(F32)
    pair_count = jnp.sum(hot, axis=1, keepdims=True)
    cross_count = jnp.sum(hot * apart, axis=1, keepdims=True)

    def two_copy(j, source):
        return copy(("two", j), source.at[part(j)], back_two.at[part(j)], swap)

    def far_copy(j):
        return copy(("far", j), with_outer.at[part(j)], turned_two.at[part(j)], me - 4)

    def one_copy(j):
        return copy(("one", j), with_cross.at[part(j)], back_one.at[part(j)], swap)

    def skew_copy(j):
        return copy(("skew", j), with_cross.at[part(j)], turned_one.at[part(j)], me + 1 - 4 * y)

    def turn_own(j):
        product(peer, part(j), 0, own, kept, half, piece)
        turned_two[part(j)] = (acc[...] * scale).astype(BF16)

    for j in range(PARTS):
        @pl.when(far_in)
        def _(j=j):
            outer_copy(j).wait_recv()
        pl.when(y == core)(lambda j=j: cross_copy_outer(j).start())
        peer_copy(j).wait_recv()

        @pl.when(upper)
        def _(j=j):
            product(peer, part(j), 0, own, kept, half, piece)
            with_own[part(j)] = (acc[...] * scale).astype(BF16)
            two_copy(j, with_own).start()

        if j < PARTS - 1:
            pl.when(lower)(lambda j=j: turn_own(j))

    far_back = upper & (me >= 4)
    skew_out = even & (lower | (me >= 3))
    skew_in = odd & (lower | (me + 3 < devices))
    @pl.when(lower)
    def _():
        for j in range(PARTS):
            product(peer, part(j), 0, outer, 0, half, piece)
            with_outer[part(j)] = (acc[...] * scale).astype(BF16)
            two_copy(j, with_outer).start()

    for j in range(PARTS):
        cross_copy_own(j).wait_recv()
    for j in range(PARTS):
        product(peer, part(j), 0, cross, 0, half, piece)
        with_cross[part(j)] = (acc[...] * scale).astype(BF16)
        pl.when(odd)(lambda j=j: one_copy(j).start())
        pl.when(skew_out)(lambda j=j: skew_copy(j).start())
    pl.when(lower)(lambda: turn_own(PARTS - 1))

    @pl.when(far_back)
    def _():
        for j in range(PARTS):
            product(peer, part(j), 0, outer, 0, half, piece)
            with_outer[part(j)] = (acc[...] * scale).astype(BF16)
            far_copy(j).start()

    passing = even & (me + 2 < devices)

    @pl.when(me + 2 < devices)
    def _():
        window_copy(2).wait_recv()

        @pl.when(even)
        def _():
            window_copy(1, window.at[1]).start()

    for j in range(PARTS):
        two_copy(j, with_own).wait_recv()
        pl.when(upper & (me + 4 < devices))(lambda j=j: far_copy(j).wait_recv())

    def settle(natural, turned, slot):
        for a in range(count):
            for b in range(count):
                ra, rb = slice(a * width, (a + 1) * width), slice(b * width, (b + 1) * width)
                tile = natural[ra, rb].astype(F32) + turned[rb, ra].astype(F32).T
                gram[a, slot * count + b] = real_only(tile, a, slot, b)

    def backward(slot):
        total = jnp.zeros((width, vectors.shape[2]), F32)
        for a in range(count):
            term = lax.dot_general(
                gram[a, slot], vectors[a], (((0,), (0,)), ((), ())), preferred_element_type=F32
            )
            at = a * slots + slot
            total = total + term * cross_count[at : at + 1]
        return total

    def terms_copy(by):
        return copy(("terms", by), terms.at[by - 1], got_terms.at[by - 1], me + by)

    def leave(by):
        for b in range(count):
            terms[by - 1, b] = backward(by * count + b).astype(BF16)
        pl.when(me + by < devices)(lambda: terms_copy(by).start())

    settle(back_two, turned_two, 2)

    leave(2)

    @pl.when(odd)
    def _():
        for j in range(PARTS):
            one_copy(j).wait_recv()
            pl.when(skew_in)(lambda j=j: skew_copy(j).wait_recv())
        settle(back_one, turned_one, 1)

    leave(1)

    @pl.loop(0, picked.shape[0])
    def _(p):
        a = jnp.clip(pairs_at[0, p] - me * count, 0, count - 1)
        b = jnp.clip(pairs_at[1, p] - me * count, 0, slots - 1)
        picked[p] = gram[a, b]

    result = pltpu.make_async_copy(picked, kblocks, out_sem)
    result.start()
    pl.when(me + 1 < devices)(lambda: window_copy(1).wait_recv())

    for a in range(count):
        total = backward(a)
        for slot in range(slots):
            column = vectors[slot] if slot < count else window[slot // count - 1, slot % count]
            at = a * slots + slot
            term = jnp.dot(gram[a, slot], column, preferred_element_type=F32)
            total = total + term * pair_count[at : at + 1]
        sums[a * width : (a + 1) * width] = total
    for by in range(1, REACH + 1):
        @pl.when(me >= by)
        def _(by=by):
            terms_copy(by).wait_recv()
            for a in range(count):
                lines = slice(a * width, (a + 1) * width)
                sums[lines] += got_terms[by - 1, a].astype(F32)
    for a in range(count):
        sigma[a] = sums[a * width : (a + 1) * width].astype(BF16)

    result.wait()
    for j in range(PARTS):
        peer_copy(j).wait_send()
        pl.when(far_out)(lambda j=j: outer_copy(j).wait_send())
        cross_copy_own(j).wait_send()
        pl.when(odd)(lambda j=j: right_copy(j).wait_send())
        two_copy(j, with_own).wait_send()
        pl.when(far_back)(lambda j=j: far_copy(j).wait_send())
        pl.when(odd)(lambda j=j: one_copy(j).wait_send())
        pl.when(skew_out)(lambda j=j: skew_copy(j).wait_send())
    for by in range(1, REACH + 1):
        pl.when(me >= 2 if by == 2 else odd | passing)(lambda by=by: window_copy(by).wait_send())
        pl.when(me >= by)(lambda by=by: mark_copy(by).wait_send())
        pl.when(me + by < devices)(lambda by=by: terms_copy(by).wait_send())


def hand_on_kernel(blocks, sigma, blocks_out, sigma_out, held, held_sigma, in_sem, out_sem):
    pieces = held.shape[0] // GROUP
    def into(j):
        if j == pieces:
            return pltpu.make_async_copy(sigma, held_sigma, in_sem.at[j])
        at = pl.ds(j * GROUP, GROUP)
        return pltpu.make_async_copy(blocks.at[at], held.at[at], in_sem.at[j])

    def out(j):
        if j == pieces:
            return pltpu.make_async_copy(held_sigma, sigma_out, out_sem.at[j])
        at = pl.ds(j * GROUP, GROUP)
        return pltpu.make_async_copy(held.at[at], blocks_out.at[at], out_sem.at[j])

    for j in range(pieces + 1):
        into(j).start()
    for j in range(pieces + 1):
        into(j).wait()
        out(j).start()
    for j in range(pieces + 1):
        out(j).wait()


def on_device(factors, block_sizes, trial_vectors, pair_list):
    count, width, depth = factors.shape
    rows = count * width
    half = depth // 2
    slots = (REACH + 1) * count
    devices = lax.axis_size("atom")
    copies = 8 * PARTS + 3 * REACH
    vmem, smem, hbm = pltpu.VMEM, pltpu.SMEM, pl.ANY
    nvec = trial_vectors.shape[2]
    npairs = pair_list.shape[0]
    turned_list = pair_list.T
    blocks, sigma = pl.pallas_call(
        functools.partial(gram_kernel, devices),
        out_shape=(
            jax.ShapeDtypeStruct((npairs, width, width), BF16),
            jax.ShapeDtypeStruct(trial_vectors.shape, BF16),
        ),
        in_specs=[pl.BlockSpec(memory_space=s) for s in (hbm, smem, vmem, vmem, smem)],
        out_specs=(pl.BlockSpec(memory_space=hbm), pl.BlockSpec(memory_space=vmem)),
        scratch_shapes=[
            pltpu.VMEM((count, slots, width, width), BF16),
            pltpu.VMEM((npairs, width, width), BF16),
            pltpu.VMEM((count, 16, width), BF16),
            pltpu.VMEM((REACH, count, 16, width), BF16),
            pltpu.VMEM((rows, depth), BF16),
            pltpu.VMEM((rows, half), BF16),
            pltpu.VMEM((rows, half), BF16),
            pltpu.VMEM((rows, half), BF16),
            pltpu.VMEM((rows, depth), BF16),
            pltpu.VMEM((REACH, count, width, nvec), BF16),
            pltpu.VMEM((rows // PARTS, rows), F32),
        ]
        + [pltpu.VMEM((rows, rows), BF16)] * 7
        + [
            pltpu.VMEM((REACH, count, width, nvec), BF16),
            pltpu.VMEM((REACH, count, width, nvec), BF16),
            pltpu.VMEM((rows, nvec), F32),
            pltpu.SemaphoreType.DMA((PARTS,)),
            pltpu.SemaphoreType.DMA,
            pltpu.SemaphoreType.DMA((copies,)),
            pltpu.SemaphoreType.DMA((copies,)),
        ],
        compiler_params=pltpu.CompilerParams(
            collective_id=0, has_side_effects=True, vmem_limit_bytes=56 * 1024 * 1024
        ),
    )(factors.reshape(rows, depth), block_sizes, trial_vectors, turned_list, turned_list)
    return pl.pallas_call(
        hand_on_kernel,
        out_shape=(
            jax.ShapeDtypeStruct(blocks.shape, BF16),
            jax.ShapeDtypeStruct(sigma.shape, BF16),
        ),
        in_specs=[pl.BlockSpec(memory_space=hbm)] * 2,
        out_specs=(pl.BlockSpec(memory_space=hbm), pl.BlockSpec(memory_space=hbm)),
        scratch_shapes=[
            pltpu.VMEM(blocks.shape, BF16),
            pltpu.VMEM(sigma.shape, BF16),
            pltpu.SemaphoreType.DMA((npairs // GROUP + 1,)),
            pltpu.SemaphoreType.DMA((npairs // GROUP + 1,)),
        ],
    )(blocks, sigma)


def solution(mesh):
    return jax.shard_map(
        on_device,
        mesh=mesh,
        in_specs=(
            P(("groups", "atom"), None, None),
            P(("groups", "atom")),
            P(("groups", "atom"), None, None),
            P(("groups", "atom"), None),
        ),
        out_specs=(P(("groups", "atom"), None, None), P(("groups", "atom"), None, None)),
        check_vma=False,
    )
```
